32 devices in a mesh: grp: 4 (over x, core), seq: 8 (over z, y).
Axes of the slice: x: 2, y: 2, z: 4, core: 2. Of those that a mesh axis runs over, the one named last changes fastest.
Arguments:
- tower_input: bfloat16 [65536, 1024], P(('grp', 'seq')), parts along dimension 0, may hold values from -6 to 6
- first_conv_taps: bfloat16 [3, 1024, 512], replicated, may hold values from -0.109375 to 0.109375
- first_conv_bias: float32 [512], replicated, may hold values from -4 to 4
- first_point_weight: bfloat16 [512, 1024], replicated, may hold values from -0.25 to 0.25
- first_point_bias: float32 [1024], replicated, may hold values from -3 to 3
- second_conv_taps: bfloat16 [3, 1024, 512], replicated, may hold values from -0.109375 to 0.109375
- second_conv_bias: float32 [512], replicated, may hold values from -4 to 4
- second_point_weight: bfloat16 [512, 1024], replicated, may hold values from -0.25 to 0.25
- second_point_bias: float32 [1024], replicated, may hold values from -3 to 3
Outputs:
- tower_out: bfloat16 [65536, 1024], P(('grp', 'seq')), parts along dimension 0
The draws below stay inside these ranges and needn't reach their ends.
There are 4 independent parts, one for each index of `grp`. The reference program is written for one: setup_inputs(seed, part) draws one part's arguments, and reference() takes and returns one part's arrays. A program takes and returns all parts, laid end to end along the dimension named above; an argument that names none is the same for every part. Nothing has to cross between parts.
All inputs are finite; a program needn't handle non-finite values.
Results may differ from the reference program's by a relative error of at most 0.01.
Values may be sent and summed in bfloat16 or wider, within the bound.
A program may use at most 128 MiB of HBM per device.

```python
import jax
import jax.numpy as jnp
from jax import lax

C = 1024
M = 512
FIRST_DILATION = 512
SECOND_DILATION = 4096
POSITIONS = 16384


def block_levels(key, shape, shards, least, largest):
    def one(axis_at, shards_of):
        steps = jax.random.uniform(jax.random.fold_in(jax.random.fold_in(key, 6), axis_at), (shards_of,), jnp.float32, least / len(shards), largest / len(shards))
        return jnp.repeat(jnp.exp(steps), shape[axis_at] // shards_of).reshape((-1,) + (1,) * (len(shape) - axis_at - 1))

    loudness = one(*shards[0])
    for cut in shards[1:]:
        loudness = loudness * one(*cut)
    return loudness


def gaussian(key, shape, scale, bound, shards=(), held_as=jnp.bfloat16):
    drawn = jax.random.normal(key, shape, jnp.float32) * scale
    if len(shards) > 0:
        drawn = block_levels(key, shape, shards, -0.22, 0.18) * drawn
    return jnp.clip(drawn, min=-bound, max=bound).astype(held_as)


def setup_inputs(seed: int = 0, part: int = 0) -> dict:
    arg_keys = jax.random.split(jax.random.key(seed), 10)
    own_keys = jax.random.split(jax.random.fold_in(arg_keys[9], part), 10)
    tower_input = gaussian(own_keys[0], (POSITIONS, C), 1.0, 6.0, ((0, 8),))
    first_conv_taps = gaussian(arg_keys[1], (3, C, M), (3 * C) ** -0.5, 0.109375)
    first_conv_bias = gaussian(arg_keys[2], (M,), 1.0, 4.0, (), jnp.float32)
    first_point_weight = gaussian(arg_keys[3], (M, C), M ** -0.5, 0.25)
    first_point_bias = gaussian(arg_keys[4], (C,), 0.5, 3.0, (), jnp.float32)
    second_conv_taps = gaussian(arg_keys[5], (3, C, M), (3 * C) ** -0.5, 0.109375)
    second_conv_bias = gaussian(arg_keys[6], (M,), 1.0, 4.0, (), jnp.float32)
    second_point_weight = gaussian(arg_keys[7], (M, C), M ** -0.5, 0.25)
    second_point_bias = gaussian(arg_keys[8], (C,), 0.5, 3.0, (), jnp.float32)
    return {"tower_input": tower_input, "first_conv_taps": first_conv_taps, "first_conv_bias": first_conv_bias, "first_point_weight": first_point_weight, "first_point_bias": first_point_bias, "second_conv_taps": second_conv_taps, "second_conv_bias": second_conv_bias, "second_point_weight": second_point_weight, "second_point_bias": second_point_bias}


def outer_term(acts, tap):
    product = jnp.dot(acts, tap, preferred_element_type=jnp.float32).astype(jnp.bfloat16)
    return lax.optimization_barrier(product).astype(jnp.float32)


def dilated_residual_layer(inputs, taps, bias_conv, point, bias_point, spacing, round_outer):
    acts = jax.nn.gelu(inputs.astype(jnp.float32)).astype(jnp.bfloat16)
    if round_outer:
        total = jnp.roll(outer_term(acts, taps[0]), spacing, axis=0)
        total = total + jnp.dot(acts, taps[1], preferred_element_type=jnp.float32)
        total = total + jnp.roll(outer_term(acts, taps[2]), -spacing, axis=0)
    else:
        total = jnp.dot(jnp.roll(acts, spacing, axis=0), taps[0], preferred_element_type=jnp.float32)
        total = total + jnp.dot(acts, taps[1], preferred_element_type=jnp.float32)
        total = total + jnp.dot(jnp.roll(acts, -spacing, axis=0), taps[2], preferred_element_type=jnp.float32)
    middle = jax.nn.gelu(total + bias_conv).astype(jnp.bfloat16)
    branch = jnp.dot(middle, point, preferred_element_type=jnp.float32)
    return (inputs.astype(jnp.float32) + branch + bias_point).astype(jnp.bfloat16)


def reference(tower_input, first_conv_taps, first_conv_bias, first_point_weight, first_point_bias, second_conv_taps, second_conv_bias, second_point_weight, second_point_bias):
    single_residual_layer = dilated_residual_layer(tower_input, first_conv_taps, first_conv_bias, first_point_weight, first_point_bias, FIRST_DILATION, False)
    return dilated_residual_layer(single_residual_layer, second_conv_taps, second_conv_bias, second_point_weight, second_point_bias, SECOND_DILATION, True)
```

```python
import jax
import jax.numpy as jnp
from jax import lax
from jax.sharding import PartitionSpec as P


def shifted(value, axis, by):
    size = lax.axis_size(axis)
    return lax.ppermute(value, axis, [(i, (i + by) % size) for i in range(size)])


def activate(values):
    return jax.nn.gelu(values.astype(jnp.float32)).astype(jnp.bfloat16)


def product(acts, tap):
    return jnp.dot(acts, tap, preferred_element_type=jnp.float32)


def rounded_product(acts, tap):
    return product(acts, tap).astype(jnp.bfloat16)


def finish(block_in, total, bias_conv, point, bias_point):
    middle = jax.nn.gelu(total + bias_conv).astype(jnp.bfloat16)
    branch = jnp.dot(middle, point, preferred_element_type=jnp.float32)
    return (block_in.astype(jnp.float32) + branch + bias_point).astype(jnp.bfloat16)


def per_device(
    tower_input,
    first_conv_taps,
    first_conv_bias,
    first_point_weight,
    first_point_bias,
    second_conv_taps,
    second_conv_bias,
    second_point_weight,
    second_point_bias,
):
    rows = tower_input.shape[0]
    d = rows // 4
    t0, t1, t2 = first_conv_taps[0], first_conv_taps[1], first_conv_taps[2]
    near = (first_conv_bias, first_point_weight, first_point_bias)
    far = (second_conv_bias, second_point_weight, second_point_bias)
    xs = [tower_input[i * d : (i + 1) * d] for i in range(4)]
    a = [activate(x) for x in xs]
    from_prev = shifted(rounded_product(a[3], t0), "seq", 1)
    from_next = shifted(rounded_product(a[0], t2), "seq", -1)

    def far_products(layer):
        acts = activate(layer)
        behind = shifted(rounded_product(acts, second_conv_taps[0]), "seq", 2)
        ahead = shifted(rounded_product(acts, second_conv_taps[2]), "seq", -2)
        return acts, behind, ahead

    def inner(i):
        total = product(a[i - 1], t0) + product(a[i], t1) + product(a[i + 1], t2)
        return finish(xs[i], total, *near)

    layers = [None] * 4
    parts = [None] * 4
    for i in (1, 2):
        layers[i] = inner(i)
        parts[i] = far_products(layers[i])
    total = product(a[0], t1) + product(a[1], t2) + from_prev.astype(jnp.float32)
    layers[0] = finish(xs[0], total, *near)
    parts[0] = far_products(layers[0])
    total = product(a[3], t1) + product(a[2], t0) + from_next.astype(jnp.float32)
    layers[3] = finish(xs[3], total, *near)
    parts[3] = far_products(layers[3])
    outs = []
    for i in range(4):
        acts, behind, ahead = parts[i]
        total = product(acts, second_conv_taps[1])
        total = total + behind.astype(jnp.float32) + ahead.astype(jnp.float32)
        outs.append(finish(layers[i], total, *far))
    return jnp.concatenate(outs, axis=0)


def solution(mesh):
    return jax.shard_map(
        per_device,
        mesh=mesh,
        in_specs=(P(("grp", "seq"), None), P(), P(), P(), P(), P(), P(), P(), P()),
        out_specs=P(("grp", "seq"), None),
        check_vma=False,
    )
```

```python
import functools

import jax
import jax.numpy as jnp
from jax import lax
from jax.experimental import pallas as pl
from jax.experimental.pallas import tpu as pltpu
from jax.sharding import PartitionSpec as P

MESH = pl.DeviceIdType.MESH
BF16 = jnp.bfloat16
F32 = jnp.float32


def gelu(v):
    return 0.5 * v * (1.0 + jnp.tanh(0.7978845608028654 * (v + 0.044715 * (v * v * v))))


def dot(a, b):
    return jnp.dot(a, b, preferred_element_type=F32)


def kernel(
    size, x_hbm, t1_hbm, b1, w1_hbm, pb1, t2_hbm, b2, w2_hbm, pb2, out_hbm,
    xv, t1, w1, t2, w2, act, halo_out, halo_in, far_out, far_in, centre,
    x_sem, t1_sem, t2_sem, w_sem, halo_send, halo_recv, far_send, far_recv, out_sem,
):
    rows = xv.shape[0]
    step = rows // 8
    d = rows // 4
    me = lax.axis_index("seq")
    fwd = [lax.rem(me + k, size) for k in (1, 2)]
    back = [lax.rem(me + size - k, size) for k in (1, 2)]

    barrier = pltpu.get_barrier_semaphore()
    for other in fwd + back:
        pl.semaphore_signal(barrier, inc=1, device_id={"seq": other}, device_id_type=MESH)

    def part(c):
        return pl.ds(pl.multiple_of(c * step, step), step)

    def load_x(c):
        return pltpu.make_async_copy(x_hbm.at[part(c)], xv.at[part(c)], x_sem.at[c])

    def load_tap(k, hbm, vmem, sem):
        return pltpu.make_async_copy(hbm.at[k], vmem.at[k], sem.at[k])

    load_w1 = pltpu.make_async_copy(w1_hbm, w1, w_sem.at[0])
    load_w2 = pltpu.make_async_copy(w2_hbm, w2, w_sem.at[1])
    load_x(0).start()
    load_tap(2, t1_hbm, t1, t1_sem).start()
    load_x(1).start()
    load_x(6).start()
    load_tap(0, t1_hbm, t1, t1_sem).start()
    load_x(7).start()
    load_x(2).start()
    load_x(4).start()
    load_tap(1, t1_hbm, t1, t1_sem).start()
    load_w1.start()
    for k in range(3):
        load_tap(k, t2_hbm, t2, t2_sem).start()
    load_x(3).start()
    load_x(5).start()
    load_w2.start()

    def halo_copy(m, j):
        return pltpu.make_async_remote_copy(
            src_ref=halo_out.at[m, j], dst_ref=halo_in.at[m, j],
            send_sem=halo_send.at[m, j], recv_sem=halo_recv.at[m, j],
            device_id={"seq": fwd[0] if m == 0 else back[0]}, device_id_type=MESH,
        )

    def far_copy(m, c):
        return pltpu.make_async_remote_copy(
            src_ref=far_out.at[m, c], dst_ref=far_in.at[m, c],
            send_sem=far_send.at[m, c], recv_sem=far_recv.at[m, c],
            device_id={"seq": fwd[1] if m == 0 else back[1]}, device_id_type=MESH,
        )

    def activate(c):
        load_x(c).wait()
        act[part(c)] = gelu(xv[part(c)].astype(F32)).astype(BF16)

    activate(0)
    load_tap(2, t1_hbm, t1, t1_sem).wait()
    pl.semaphore_wait(barrier, 4)
    for m in (1, 0):
        tap = 2 * m
        first = 0 if m == 1 else 6
        if m == 0:
            load_tap(tap, t1_hbm, t1, t1_sem).wait()

        @pl.loop(0, 2)
        def _(j):
            if m == 0:
                activate(first + j)
            else:
                @pl.when(j == 1)
                def _():
                    activate(first + j)
            halo_out[m, j] = dot(act[part(first + j)], t1[tap]).astype(BF16)
            halo_copy(m, j).start()

    def layer(c, total):
        middle = gelu(total + b1[...]).astype(BF16)
        one = (xv[part(c)].astype(F32) + dot(middle, w1[...]) + pb1[...]).astype(BF16)
        xv[part(c)] = one
        far_act = gelu(one.astype(F32)).astype(BF16)
        far_out[0, c] = dot(far_act, t2[0]).astype(BF16)
        far_copy(0, c).start()
        far_out[1, c] = dot(far_act, t2[2]).astype(BF16)
        far_copy(1, c).start()
        centre[part(c)] = dot(far_act, t2[1])

    activate(2)
    activate(4)
    load_tap(1, t1_hbm, t1, t1_sem).wait()
    load_w1.wait()
    for k in range(3):
        load_tap(k, t2_hbm, t2, t2_sem).wait()

    @pl.loop(0, 4)
    def _(i):
        j, m = i // 2, lax.rem(i, 2)
        c = 2 + j + 2 * m
        layer(c, dot(act[part(c - 2)], t1[0]) + dot(act[part(c)], t1[1]) + dot(act[part(c + 2)], t1[2]))

        @pl.when(i == 1)
        def _():
            activate(3)
            activate(5)

    @pl.loop(0, 4)
    def _(i):
        j, m = i // 2, lax.rem(i, 2)
        c = 6 * m + j
        near = dot(act[part(c)], t1[1]) + dot(act[part(c + 2 - 4 * m)], t1[2 - 2 * m])

        @pl.when(m == 0)
        def _():
            halo_copy(0, j).wait_recv()

        @pl.when(m == 1)
        def _():
            halo_copy(1, j).wait_recv()

        layer(c, near + halo_in[m, j].astype(F32))

    load_w2.wait()

    def finish(c):
        far_copy(0, c).wait_recv()
        far_copy(1, c).wait_recv()
        total = centre[part(c)] + far_in[0, c].astype(F32) + far_in[1, c].astype(F32)
        middle = gelu(total + b2[...]).astype(BF16)
        xv[part(c)] = (xv[part(c)].astype(F32) + dot(middle, w2[...]) + pb2[...]).astype(BF16)
        pltpu.make_async_copy(xv.at[part(c)], out_hbm.at[part(c)], out_sem.at[c]).start()

    @pl.loop(0, 8)
    def _(i):
        edge = i // 4
        k = lax.rem(i, 4)
        j, m = k // 2, lax.rem(k, 2)
        finish(j + (1 - edge) * (2 + 2 * m) + edge * 6 * m)

    for m in range(2):
        for j in range(2):
            halo_copy(m, j).wait_send()

    @pl.loop(0, 8)
    def _(c):
        far_copy(0, c).wait_send()
        far_copy(1, c).wait_send()
        pltpu.make_async_copy(xv.at[part(c)], out_hbm.at[part(c)], out_sem.at[c]).wait()


def per_device(x, t1, b1, w1, pb1, t2, b2, w2, pb2):
    rows, wide = x.shape
    mid = w1.shape[0]
    step = rows // 8
    hbm = pl.BlockSpec(memory_space=pl.ANY)
    vmem = pl.BlockSpec(memory_space=pltpu.VMEM)
    dma = pltpu.SemaphoreType.DMA
    flops = 2 * rows * wide * mid * 8
    return pl.pallas_call(
        functools.partial(kernel, lax.axis_size("seq")),
        out_shape=jax.ShapeDtypeStruct((rows, wide), BF16),
        in_specs=[hbm, hbm, vmem, hbm, vmem, hbm, vmem, hbm, vmem],
        out_specs=hbm,
        scratch_shapes=[
            pltpu.VMEM((rows, wide), BF16),
            pltpu.VMEM((3, wide, mid), BF16),
            pltpu.VMEM((mid, wide), BF16),
            pltpu.VMEM((3, wide, mid), BF16),
            pltpu.VMEM((mid, wide), BF16),
            pltpu.VMEM((rows, wide), BF16),
            pltpu.VMEM((2, 2, step, mid), BF16),
            pltpu.VMEM((2, 2, step, mid), BF16),
            pltpu.VMEM((2, 8, step, mid), BF16),
            pltpu.VMEM((2, 8, step, mid), BF16),
            pltpu.VMEM((rows, mid), F32),
            dma((8,)), dma((3,)), dma((3,)), dma((2,)),
            dma((2, 2)), dma((2, 2)), dma((2, 8)), dma((2, 8)), dma((8,)),
        ],
        compiler_params=pltpu.CompilerParams(
            collective_id=0, has_side_effects=True, vmem_limit_bytes=56 * 2**20
        ),
        cost_estimate=pl.CostEstimate(flops=flops, bytes_accessed=16 * 2**20, transcendentals=0),
    )(x, t1, b1.reshape(1, mid), w1, pb1.reshape(1, wide), t2, b2.reshape(1, mid), w2, pb2.reshape(1, wide))


def solution(mesh):
    return jax.shard_map(
        per_device,
        mesh=mesh,
        in_specs=(P(("grp", "seq"), None), P(), P(), P(), P(), P(), P(), P(), P()),
        out_specs=P(("grp", "seq"), None),
        check_vma=False,
    )
```
